32 devices in a mesh: grp: 4 (over y, core), feat: 8 (over z, x).
Axes of the slice: x: 2, y: 2, z: 4, core: 2. Of those that a mesh axis runs over, the one named last changes fastest.
Arguments:
- features: bfloat16 [128, 16384], P('feat', 'grp'), may hold values from -6 to 6
- w_self: bfloat16 [128, 256], replicated, may hold values from -0.5 to 0.5
- w_neigh: bfloat16 [128, 256], replicated, may hold values from -0.5 to 0.5
- bias: float32 [256], replicated, may hold values from -3 to 3
- tile_vals: bfloat16 [4, 8, 8, 128, 128], P('grp'), may hold values from -0.5 to 0.5
- tile_src: int32 [4, 8, 8], P('grp'), may hold values from 0 to 39, as said below
- tile_dst: int32 [4, 8, 8], P('grp'), may hold values from 0 to 3
- tile_count: int32 [4, 8], P('grp'), may hold values from 1 to 8, as said below
- hub_blocks: int32 [4, 2], P('grp'), may hold values from 0 to 31, as said below
- cotangent: bfloat16 [16384, 256], P(('grp', 'feat')), may hold values from -6 to 6
Outputs:
- output: bfloat16 [16384, 256], P(('grp', 'feat'))
- feat_grad: float32 [128, 16384], P('feat', 'grp')
- wself_grad: float32 [128, 256], P('feat')
- wneigh_grad: float32 [128, 256], P('feat')
- bias_grad: float32 [256], replicated
The draws below stay inside these ranges and needn't reach their ends.
Inputs may be any that keep to these rules, and one draw needn't show every extreme that they name: `tile_src`: a slot number of the tile's own group's blocks below 32, or 32 plus a hub number. `tile_count`: some owner uses all 8 slots in every draw. `hub_blocks`: the 2 block numbers of a group are distinct.
All inputs are finite; a program needn't handle non-finite values.
Results may differ from the reference program's by a relative error of at most 0.0055.
Values may be sent and summed in bfloat16 or wider, within the bound.
A program may use at most 128 MiB of HBM per device.

```python
import jax
import jax.numpy as jnp

F = 128
H = 256
B = 128
NB_DEV = 4
HUBG = 2
TCAP = 8
GROUPS = 4
OWNERS = 8
NODES = 16384


def draw_tile_src(key, part):
    shape = (GROUPS, OWNERS, TCAP)
    coin = jax.random.randint(jax.random.fold_in(key, 11), shape, 0, 2)
    local_ids = jax.random.randint(jax.random.fold_in(key, 12), shape, 0, OWNERS * NB_DEV)
    hub_ids = jax.random.randint(jax.random.fold_in(key, 13), shape, 0, GROUPS * HUBG) + OWNERS * NB_DEV
    return jnp.where(coin == 1, hub_ids, local_ids).astype(jnp.int32)


def draw_tile_count(key, part):
    counts = jax.random.randint(jax.random.fold_in(key, 21), (GROUPS * OWNERS,), 1, TCAP + 1)
    filled = jax.random.randint(jax.random.fold_in(key, 22), (), 0, GROUPS * OWNERS)
    counts = jnp.where(jnp.arange(GROUPS * OWNERS, dtype=jnp.int32) == filled, TCAP, counts)
    return counts.reshape(GROUPS, OWNERS).astype(jnp.int32)


def draw_hub_blocks(key, part):
    total = OWNERS * NB_DEV
    keys = jax.random.split(jax.random.fold_in(key, 31), GROUPS)
    orders = jax.vmap(lambda single: jax.random.permutation(single, total))(keys).astype(jnp.int32)
    group_ids = jnp.arange(GROUPS, dtype=jnp.int32)
    leading = orders[:, 0]
    target = jnp.where(group_ids == 0, total - 1, jnp.where(group_ids == 1, 0, leading))
    shifted = (orders + (target - leading)[:, None] + total) % total
    return shifted[:, :HUBG].astype(jnp.int32)


def plant(drawn, own_key, smallest, largest):
    spot = [jax.random.randint(jax.random.fold_in(own_key, axis), (), 0, length) for axis, length in enumerate(drawn.shape)]
    main_axis = drawn.shape.index(max(drawn.shape))
    beside = spot[:main_axis] + [(spot[main_axis] + 1) % drawn.shape[main_axis]] + spot[main_axis + 1:]
    return drawn.at[tuple(spot)].set(smallest).at[tuple(beside)].set(largest)


def shard_levels(stream_key, extent, cuts, low, high):
    level, own = 1.0, jax.random.fold_in(stream_key, 6)
    for axis_at, shards_of in cuts:
        heights = jnp.exp(jax.random.uniform(jax.random.fold_in(own, axis_at), (shards_of,), jnp.float32, low / len(cuts), high / len(cuts)))
        level = level * jnp.repeat(heights, extent[axis_at] // shards_of).reshape([-1 if axis == axis_at else 1 for axis in range(len(extent))])
    return level


def centred(own_key, dims, width, bound, cuts=(), kind=jnp.bfloat16):
    array = jax.random.normal(own_key, dims, jnp.float32) * width
    if len(cuts) > 0:
        array = shard_levels(own_key, dims, cuts, -0.22, 0.18) * array
    return jnp.clip(array, min=-bound, max=bound).astype(kind)


def setup_inputs(seed: int = 0) -> dict:
    seeds = jax.random.split(jax.random.key(seed), 11)
    features = centred(seeds[0], (F, NODES), 1.0, 6.0, ((0, 8), (1, 4)))
    w_self = centred(seeds[1], (F, H), F ** -0.5, 0.5)
    w_neigh = centred(seeds[2], (F, H), F ** -0.5, 0.5)
    bias = centred(seeds[3], (H,), 0.5, 3.0, (), jnp.float32)
    tile_vals = centred(seeds[4], (GROUPS, OWNERS, TCAP, B, B), B ** -0.5, 0.5, ((0, 4),))
    tile_src = draw_tile_src(jax.random.fold_in(seeds[10], 71), 0)
    tile_dst = plant(jax.random.randint(seeds[6], (GROUPS, OWNERS, TCAP), 0, NB_DEV), jax.random.fold_in(seeds[6], 1), 0, NB_DEV - 1).astype(jnp.int32)
    tile_count = draw_tile_count(jax.random.fold_in(seeds[10], 71), 0)
    hub_blocks = draw_hub_blocks(jax.random.fold_in(seeds[10], 71), 0)
    cotangent = centred(seeds[9], (NODES, H), 1.0, 6.0, ((0, 32),))
    return {"features": features, "w_self": w_self, "w_neigh": w_neigh, "bias": bias, "tile_vals": tile_vals, "tile_src": tile_src, "tile_dst": tile_dst, "tile_count": tile_count, "hub_blocks": hub_blocks, "cotangent": cotangent}


def silu_parts(preact):
    sig = jax.nn.sigmoid(preact)
    return preact * sig, sig * (1.0 + preact * (1.0 - sig))


def reference(features, w_self, w_neigh, bias, tile_vals, tile_src, tile_dst, tile_count, hub_blocks, cotangent):
    gblk = OWNERS * NB_DEV
    hub_total = GROUPS * HUBG
    xrows = features.T
    blocks = xrows.reshape(GROUPS, gblk, B, F)
    group_ids = jnp.arange(GROUPS, dtype=jnp.int32)[:, None]
    hubs = blocks[group_ids, hub_blocks].reshape(hub_total, B, F)
    slots = jnp.concatenate([blocks, jnp.broadcast_to(hubs[None], (GROUPS, hub_total, B, F))], axis=1)
    picked = slots[group_ids[:, :, None], tile_src]
    live_slots = (jnp.arange(TCAP, dtype=jnp.int32)[None, None, :] < tile_count[:, :, None]).astype(jnp.float32)
    values = tile_vals.astype(jnp.float32)
    contrib = jnp.einsum('gotds,gotsf->gotdf', values, picked.astype(jnp.float32)) * live_slots[..., None, None]
    dst_hot = (tile_dst[..., None] == jnp.arange(NB_DEV, dtype=jnp.int32)).astype(jnp.float32)
    agg = jnp.einsum('gotdf,gotn->gondf', contrib, dst_hot).reshape(GROUPS * gblk * B, F).astype(jnp.bfloat16)
    preact = jnp.dot(xrows, w_self, preferred_element_type=jnp.float32) + jnp.dot(agg, w_neigh, preferred_element_type=jnp.float32) + bias
    activated, slope = silu_parts(preact)
    output = activated.astype(jnp.bfloat16)
    grad_pre = (cotangent.astype(jnp.float32) * slope).astype(jnp.bfloat16)
    wself_grad = jnp.dot(xrows.T, grad_pre, preferred_element_type=jnp.float32)
    wneigh_grad = jnp.dot(agg.T, grad_pre, preferred_element_type=jnp.float32)
    bias_grad = jnp.sum(grad_pre.astype(jnp.float32), axis=0)
    self_grad = jnp.dot(grad_pre, w_self.T, preferred_element_type=jnp.float32)
    agg_grad = jnp.dot(grad_pre, w_neigh.T, preferred_element_type=jnp.float32).astype(jnp.bfloat16)
    agg_blocks = agg_grad.reshape(GROUPS, OWNERS, NB_DEV, B, F).astype(jnp.float32)
    chosen = jnp.einsum('gondf,gotn->gotdf', agg_blocks, dst_hot)
    src_grad = jnp.einsum('gotds,gotdf->gotsf', values, chosen) * live_slots[..., None, None]
    slot_grad = jnp.zeros((GROUPS, gblk + hub_total, B, F), jnp.float32).at[group_ids[:, :, None], tile_src].add(src_grad)
    local_grad = slot_grad[:, :gblk]
    hub_grad = jnp.sum(slot_grad[:, gblk:], axis=0).reshape(GROUPS, HUBG, B, F)
    local_grad = local_grad.at[group_ids, hub_blocks].add(hub_grad)
    feat_grad = (self_grad + local_grad.reshape(GROUPS * gblk * B, F)).T
    return output, feat_grad, wself_grad, wneigh_grad, bias_grad
```

```python
import functools

import jax
import jax.numpy as jnp
from jax import lax
from jax.experimental import pallas as pl
from jax.experimental.pallas import tpu as pltpu
from jax.sharding import PartitionSpec as P


def lanes(index, width):
    return pl.ds(pl.multiple_of(index * width, width), width)


def gather_tiles(own_blocks, src_ref, dst_ref, x_ref, tiles_ref, out_ref):
    owners, slots, size, _ = tiles_ref.shape
    rows = x_ref.shape[0]

    def owner(o, carry):
        total = jnp.zeros((own_blocks * rows, size), jnp.float32)
        for t in range(slots):
            x = x_ref[:, lanes(src_ref[o * slots + t], size)].astype(jnp.float32)
            dst = dst_ref[o * slots + t]
            left = jnp.concatenate(
                [x * (dst == d).astype(jnp.float32) for d in range(own_blocks)], axis=0
            ).astype(jnp.bfloat16)
            total += lax.dot_general(
                left, tiles_ref[o, t], (((1,), (1,)), ((), ())), preferred_element_type=jnp.float32
            )
        for d in range(own_blocks):
            out_ref[:, lanes(o * own_blocks + d, size)] = total[d * rows : (d + 1) * rows].astype(
                out_ref.dtype
            )
        return carry

    lax.fori_loop(0, owners, owner, 0)


def scatter_tiles(own_blocks, src_ref, dst_ref, g_ref, tiles_ref, self_ref, out_ref, hub_ref, total):
    owners, slots, size, _ = tiles_ref.shape
    nodes = g_ref.shape[1]
    total[:, :nodes] = self_ref[...].astype(jnp.float32)
    total[:, nodes:] = jnp.zeros((total.shape[0], total.shape[1] - nodes), jnp.float32)

    def owner(o, carry):
        terms = []
        for t in range(slots):
            dst = dst_ref[o * slots + t]
            g = g_ref[:, lanes(o * own_blocks + jnp.maximum(dst, 0), size)]
            term = jnp.dot(g, tiles_ref[o, t], preferred_element_type=jnp.float32)
            terms.append(term * (dst >= 0).astype(jnp.float32))
        for t in range(slots):
            at = lanes(src_ref[o * slots + t], size)
            total[:, at] = total[:, at] + terms[t]
        return carry

    lax.fori_loop(0, owners, owner, 0)
    out_ref[...] = total[:, :nodes]
    hub_ref[...] = total[:, nodes:].astype(hub_ref.dtype)


def add_hubs(ids_ref, part_ref, hub_ref, out_ref):
    peers, _, width = hub_ref.shape
    hubs = ids_ref.shape[0]
    size = width // hubs
    out_ref[...] = part_ref[...]
    back = hub_ref[0].astype(jnp.float32)
    for p in range(1, peers):
        back += hub_ref[p].astype(jnp.float32)
    for k in range(hubs):
        at = lanes(ids_ref[k], size)
        out_ref[:, at] = out_ref[:, at] + back[:, k * size : (k + 1) * size]


def local(
    features,
    w_self,
    w_neigh,
    bias,
    tile_vals,
    tile_src,
    tile_dst,
    tile_count,
    hub_blocks,
    cotangent,
):
    columns, nodes = features.shape
    owners = lax.axis_size("feat")
    position = lax.axis_index("feat")
    size = tile_vals.shape[-1]
    slots = tile_src.shape[2]
    own_blocks = nodes // size // owners
    hubs = hub_blocks.shape[1]
    rows = max(columns, 16)
    vmem, smem = pl.BlockSpec(memory_space=pltpu.VMEM), pl.BlockSpec(memory_space=pltpu.SMEM)
    params = pltpu.CompilerParams(vmem_limit_bytes=40 * 1024 * 1024)

    def padded(a):
        return a if rows == columns else jnp.pad(a, ((0, rows - columns), (0, 0)))

    own_hubs = jnp.concatenate(
        [lax.dynamic_slice_in_dim(features, hub_blocks[0, k] * size, size, 1) for k in range(hubs)],
        axis=1,
    )
    all_hubs = lax.all_gather(own_hubs, "grp", axis=1, tiled=True)
    combined = padded(jnp.concatenate([features, all_hubs], axis=1))
    live = jnp.arange(slots, dtype=jnp.int32)[None, :] < tile_count[0][:, None]
    src = tile_src[0].reshape(-1)
    dst = jnp.where(live, tile_dst[0], -1).reshape(-1)
    tiles = tile_vals[0]
    agg = pl.pallas_call(
        functools.partial(gather_tiles, own_blocks),
        out_shape=jax.ShapeDtypeStruct((rows, nodes), jnp.bfloat16),
        in_specs=[smem, smem, vmem, vmem],
        out_specs=vmem,
        compiler_params=params,
        name="gather_tiles",
    )(src, dst, combined, tiles)[:columns]
    both = lax.all_to_all(
        jnp.stack([features, agg]), "feat", split_axis=2, concat_axis=1, tiled=True
    )
    both = both.reshape(-1, both.shape[2])
    weights = jnp.concatenate([w_self, w_neigh], axis=0)
    preact = (
        lax.dot_general(both, weights, (((0,), (0,)), ((), ())), preferred_element_type=jnp.float32)
        + bias
    )
    sig = jax.nn.sigmoid(preact)
    output = (preact * sig).astype(jnp.bfloat16)
    slope = sig * (1.0 + preact * (1.0 - sig))
    grad_pre = (cotangent.astype(jnp.float32) * slope).astype(jnp.bfloat16)
    grads = lax.dot_general(
        weights, grad_pre, (((1,), (1,)), ((), ())), preferred_element_type=jnp.float32
    ).astype(jnp.bfloat16)
    back = lax.all_to_all(
        grads.reshape(2, -1, grads.shape[1]), "feat", split_axis=1, concat_axis=2, tiled=True
    )
    weight_part = jnp.dot(both, grad_pre, preferred_element_type=jnp.float32)
    bias_part = jnp.sum(grad_pre.astype(jnp.float32), axis=0)
    weight_sum, bias_grad = lax.psum((weight_part, bias_part), ("grp", "feat"))
    weight_sum = lax.dynamic_slice_in_dim(
        weight_sum.reshape(2, -1, weight_sum.shape[1]), position * columns, columns, 1
    )
    part, hub_part = pl.pallas_call(
        functools.partial(scatter_tiles, own_blocks),
        out_shape=(
            jax.ShapeDtypeStruct((rows, nodes), jnp.float32),
            jax.ShapeDtypeStruct((rows, combined.shape[1] - nodes), jnp.bfloat16),
        ),
        in_specs=[smem, smem, vmem, vmem, vmem],
        out_specs=(vmem, vmem),
        scratch_shapes=[pltpu.VMEM((rows, combined.shape[1]), jnp.float32)],
        compiler_params=params,
        name="scatter_tiles",
    )(src, dst, padded(back[1]), tiles, padded(back[0]))
    hub_back = lax.all_to_all(
        hub_part[None, :columns], "grp", split_axis=2, concat_axis=0, tiled=True
    )
    feat_grad = pl.pallas_call(
        add_hubs,
        out_shape=jax.ShapeDtypeStruct((columns, nodes), jnp.float32),
        in_specs=[smem, vmem, vmem],
        out_specs=vmem,
        compiler_params=params,
        name="add_hubs",
    )(hub_blocks[0], part[:columns], hub_back)
    return (output, feat_grad, weight_sum[0], weight_sum[1], bias_grad)


def solution(mesh):
    return jax.shard_map(
        local,
        mesh=mesh,
        in_specs=(
            P("feat", "grp"),
            P(),
            P(),
            P(),
            P("grp", None, None, None, None),
            P("grp", None, None),
            P("grp", None, None),
            P("grp", None),
            P("grp", None),
            P(("grp", "feat"), None),
        ),
        out_specs=(
            P(("grp", "feat"), None),
            P("feat", "grp"),
            P("feat", None),
            P("feat", None),
            P(),
        ),
        check_vma=False,
    )
```

```python
import functools

import jax
import jax.numpy as jnp
from jax import lax
from jax.experimental import pallas as pl
from jax.experimental.pallas import tpu as pltpu
from jax.sharding import PartitionSpec as P


def lanes(index, width):
    return pl.ds(pl.multiple_of(index * width, width), width)


def gather_tiles(own_blocks, src_ref, dst_ref, x_ref, tiles_ref, out_ref):
    owners, slots, size, _ = tiles_ref.shape
    rows = x_ref.shape[0]
    out_ref[:rows, :] = x_ref[:, : out_ref.shape[1]]

    def owner(o, carry):
        total = jnp.zeros((own_blocks * rows, size), jnp.float32)
        for t in range(slots):
            x = x_ref[:, lanes(src_ref[o * slots + t], size)].astype(jnp.float32)
            dst = dst_ref[o * slots + t]
            left = jnp.concatenate(
                [x * (dst == d).astype(jnp.float32) for d in range(own_blocks)], axis=0
            ).astype(jnp.bfloat16)
            total += lax.dot_general(
                left, tiles_ref[o, t], (((1,), (1,)), ((), ())), preferred_element_type=jnp.float32
            )
        for d in range(own_blocks):
            out_ref[rows:, lanes(o * own_blocks + d, size)] = total[d * rows : (d + 1) * rows].astype(
                out_ref.dtype
            )
        return carry

    lax.fori_loop(0, owners, owner, 0)


def scatter_tiles(own_blocks, src_ref, dst_ref, g_ref, tiles_ref, out_ref, hub_ref, total):
    owners, slots, size, _ = tiles_ref.shape
    rows, nodes = out_ref.shape
    total[:, :nodes] = g_ref[:rows, :].astype(jnp.float32)
    total[:, nodes:] = jnp.zeros((total.shape[0], total.shape[1] - nodes), jnp.float32)

    def owner(o, carry):
        terms = []
        for t in range(slots):
            dst = dst_ref[o * slots + t]
            g = g_ref[rows:, lanes(o * own_blocks + jnp.maximum(dst, 0), size)]
            term = jnp.dot(g, tiles_ref[o, t], preferred_element_type=jnp.float32)
            terms.append(term * (dst >= 0).astype(jnp.float32))
        for t in range(slots):
            at = lanes(src_ref[o * slots + t], size)
            total[:, at] = total[:, at] + terms[t]
        return carry

    lax.fori_loop(0, owners, owner, 0)
    out_ref[...] = total[:, :nodes]
    hub_ref[...] = total[:, nodes:].astype(hub_ref.dtype)


def add_hubs(ids_ref, part_ref, hub_ref, out_ref):
    peers, _, width = hub_ref.shape
    hubs = ids_ref.shape[0]
    size = width // hubs
    out_ref[...] = part_ref[...]
    back = hub_ref[0].astype(jnp.float32)
    for p in range(1, peers):
        back += hub_ref[p].astype(jnp.float32)
    for k in range(hubs):
        at = lanes(ids_ref[k], size)
        out_ref[:, at] = out_ref[:, at] + back[:, k * size : (k + 1) * size]


def exchange_body(axis, cuts, joins, *refs):
    items = len(cuts)
    inputs, outputs, held = refs[:items], refs[items : 2 * items], refs[2 * items : 3 * items]
    send_sem, recv_sem = refs[3 * items :]
    peers = lax.axis_size(axis)
    me = lax.axis_index(axis)

    def block(i, peer):
        if cuts[i] == "whole":
            return inputs[i]
        if cuts[i] == "lead":
            return inputs[i].at[peer]
        return inputs[i].at[:, lanes(peer, held[i].shape[2])]

    others = [lax.rem(me + step, peers) for step in range(1, peers)]
    barrier = pltpu.get_barrier_semaphore()
    for peer in others:
        pl.semaphore_signal(
            barrier, inc=1, device_id={axis: peer}, device_id_type=pl.DeviceIdType.MESH
        )
    pl.semaphore_wait(barrier, peers - 1)
    copies = []
    for step, peer in enumerate(others):
        for i in range(items):
            copy = pltpu.make_async_remote_copy(
                src_ref=block(i, peer),
                dst_ref=held[i].at[me],
                send_sem=send_sem.at[i, step],
                recv_sem=recv_sem.at[i, step],
                device_id={axis: peer},
                device_id_type=pl.DeviceIdType.MESH,
            )
            copy.start()
            copies.append(copy)
    for i in range(items):
        held[i][me] = block(i, me)[...]
    for copy in copies:
        copy.wait()
    for i in range(items):
        if joins[i] == "sum":
            total = held[i][0]
            for p in range(1, peers):
                total += held[i][p]
            outputs[i][...] = total
        elif joins[i] == "lanes":
            width = held[i].shape[2]
            for p in range(peers):
                outputs[i][:, p * width : (p + 1) * width] = held[i][p]
        else:
            outputs[i][...] = held[i][...]


def exchange(axis, number, arrays, cuts, joins):
    peers = lax.axis_size(axis)
    blocks, outs = [], []
    for array, cut, join in zip(arrays, cuts, joins):
        if cut == "lead":
            rows, width = array.shape[1:]
        else:
            rows, width = array.shape
            width = width // peers if cut == "lanes" else width
        blocks.append(pltpu.VMEM((peers, rows, width), array.dtype))
        shape = {"sum": (rows, width), "lanes": (rows, peers * width)}.get(join, (peers, rows, width))
        outs.append(jax.ShapeDtypeStruct(shape, array.dtype))
    vmem = pl.BlockSpec(memory_space=pltpu.VMEM)
    semaphores = pltpu.SemaphoreType.DMA((len(arrays), peers - 1))
    return pl.pallas_call(
        functools.partial(exchange_body, axis, cuts, joins),
        out_shape=outs,
        in_specs=[vmem] * len(arrays),
        out_specs=[vmem] * len(arrays),
        scratch_shapes=[*blocks, semaphores, semaphores],
        compiler_params=pltpu.CompilerParams(
            collective_id=number, has_side_effects=True, vmem_limit_bytes=40 * 1024 * 1024
        ),
        name=f"exchange_{number}",
    )(*arrays)


def local(
    features,
    w_self,
    w_neigh,
    bias,
    tile_vals,
    tile_src,
    tile_dst,
    tile_count,
    hub_blocks,
    cotangent,
):
    columns, nodes = features.shape
    owners = lax.axis_size("feat")
    size = tile_vals.shape[-1]
    slots = tile_src.shape[2]
    own_blocks = nodes // size // owners
    hubs = hub_blocks.shape[1]
    hidden = w_self.shape[1]
    rows = max(columns, 16)
    vmem, smem = pl.BlockSpec(memory_space=pltpu.VMEM), pl.BlockSpec(memory_space=pltpu.SMEM)
    params = pltpu.CompilerParams(vmem_limit_bytes=40 * 1024 * 1024)

    def padded(a):
        spare = [(0, 0)] * a.ndim
        spare[-2] = (0, rows - columns)
        return a if rows == columns else jnp.pad(a, spare)

    mine = padded(features)
    own_hubs = jnp.concatenate(
        [lax.dynamic_slice_in_dim(mine, hub_blocks[0, k] * size, size, 1) for k in range(hubs)],
        axis=1,
    )
    (all_hubs,) = exchange("grp", 0, [own_hubs], ["whole"], ["lanes"])
    combined = jnp.concatenate([mine, all_hubs], axis=1)
    live = jnp.arange(slots, dtype=jnp.int32)[None, :] < tile_count[0][:, None]
    src = tile_src[0].reshape(-1)
    dst = jnp.where(live, tile_dst[0], -1).reshape(-1)
    tiles = tile_vals[0]
    both = pl.pallas_call(
        functools.partial(gather_tiles, own_blocks),
        out_shape=jax.ShapeDtypeStruct((2 * rows, nodes), jnp.bfloat16),
        in_specs=[smem, smem, vmem, vmem],
        out_specs=vmem,
        compiler_params=params,
        name="gather_tiles",
    )(src, dst, combined, tiles)
    (both,) = exchange("feat", 1, [both], ["lanes"], ["lead"])
    both = both.reshape(owners * 2 * rows, nodes // owners)
    weights = jnp.stack(
        [padded(w.reshape(owners, columns, hidden)) for w in (w_self, w_neigh)], axis=1
    ).reshape(owners * 2 * rows, hidden)
    preact = (
        lax.dot_general(both, weights, (((0,), (0,)), ((), ())), preferred_element_type=jnp.float32)
        + bias
    )
    sig = jax.nn.sigmoid(preact)
    output = (preact * sig).astype(jnp.bfloat16)
    slope = sig * (1.0 + preact * (1.0 - sig))
    grad_pre = (cotangent.astype(jnp.float32) * slope).astype(jnp.bfloat16)
    grads = lax.dot_general(
        weights, grad_pre, (((1,), (1,)), ((), ())), preferred_element_type=jnp.float32
    ).astype(jnp.bfloat16)
    weight_part = jnp.dot(both, grad_pre, preferred_element_type=jnp.float32)
    bias_part = jnp.sum(grad_pre.astype(jnp.float32), axis=0)
    sums = jnp.concatenate(
        [
            weight_part.reshape(owners, 2 * rows, hidden),
            jnp.broadcast_to(bias_part, (owners, 8, hidden)),
        ],
        axis=1,
    )
    back, sums = exchange(
        "feat",
        2,
        [grads.reshape(owners, 2 * rows, nodes // owners), sums],
        ["lead", "lead"],
        ["lanes", "sum"],
    )
    part, hub_part = pl.pallas_call(
        functools.partial(scatter_tiles, own_blocks),
        out_shape=(
            jax.ShapeDtypeStruct((rows, nodes), jnp.float32),
            jax.ShapeDtypeStruct((rows, combined.shape[1] - nodes), jnp.bfloat16),
        ),
        in_specs=[smem, smem, vmem, vmem],
        out_specs=(vmem, vmem),
        scratch_shapes=[pltpu.VMEM((rows, combined.shape[1]), jnp.float32)],
        compiler_params=params,
        name="scatter_tiles",
    )(src, dst, back, tiles)
    hub_back, sums = exchange("grp", 3, [hub_part, sums], ["lanes", "whole"], ["lead", "sum"])
    feat_grad = pl.pallas_call(
        add_hubs,
        out_shape=jax.ShapeDtypeStruct((columns, nodes), jnp.float32),
        in_specs=[smem, vmem, vmem],
        out_specs=vmem,
        compiler_params=params,
        name="add_hubs",
    )(hub_blocks[0], part[:columns], hub_back[:, :columns])
    return (
        output,
        feat_grad,
        sums[:columns],
        sums[rows : rows + columns],
        sums[2 * rows],
    )


def solution(mesh):
    return jax.shard_map(
        local,
        mesh=mesh,
        in_specs=(
            P("feat", "grp"),
            P(),
            P(),
            P(),
            P("grp", None, None, None, None),
            P("grp", None, None),
            P("grp", None, None),
            P("grp", None),
            P("grp", None),
            P(("grp", "feat"), None),
        ),
        out_specs=(
            P(("grp", "feat"), None),
            P("feat", "grp"),
            P("feat", None),
            P("feat", None),
            P(),
        ),
        check_vma=False,
    )
```

```python
import functools

import jax
import jax.numpy as jnp
from jax import lax
from jax.experimental import pallas as pl
from jax.experimental.pallas import tpu as pltpu
from jax.sharding import PartitionSpec as P


def lanes(index, width):
    return pl.ds(pl.multiple_of(index * width, width), width)


def destination(dst_ref, count_ref, o, t):
    return jnp.where(t < count_ref[0, o], dst_ref[0, o, t], -1)


def gather_tiles(
    own_blocks, src_ref, dst_ref, count_ref, features_ref, hubs_ref, tiles_ref, out_ref, x_ref
):
    _, owners, slots, size, _ = tiles_ref.shape
    rows = x_ref.shape[0]
    nodes = out_ref.shape[1]
    out_ref[:rows, :] = features_ref[...]
    x_ref[:, :nodes] = features_ref[...]
    x_ref[:, nodes:] = hubs_ref[...]

    def owner(o, carry):
        total = jnp.zeros((own_blocks * rows, size), jnp.float32)
        for t in range(slots):
            x = x_ref[:, lanes(src_ref[0, o, t], size)].astype(jnp.float32)
            dst = destination(dst_ref, count_ref, o, t)
            left = jnp.concatenate(
                [x * (dst == d).astype(jnp.float32) for d in range(own_blocks)], axis=0
            ).astype(jnp.bfloat16)
            total += lax.dot_general(
                left, tiles_ref[0, o, t], (((1,), (1,)), ((), ())), preferred_element_type=jnp.float32
            )
        for d in range(own_blocks):
            out_ref[rows:, lanes(o * own_blocks + d, size)] = total[d * rows : (d + 1) * rows].astype(
                out_ref.dtype
            )
        return carry

    lax.fori_loop(0, owners, owner, 0)


def scatter_tiles(own_blocks, src_ref, dst_ref, count_ref, g_ref, tiles_ref, out_ref, hub_ref, total):
    _, owners, slots, size, _ = tiles_ref.shape
    rows, nodes = out_ref.shape
    total[:, :nodes] = g_ref[:rows, :].astype(jnp.float32)
    total[:, nodes:] = jnp.zeros((total.shape[0], total.shape[1] - nodes), jnp.float32)

    def owner(o, carry):
        terms = []
        for t in range(slots):
            dst = destination(dst_ref, count_ref, o, t)
            g = g_ref[rows:, lanes(o * own_blocks + jnp.maximum(dst, 0), size)]
            term = jnp.dot(g, tiles_ref[0, o, t], preferred_element_type=jnp.float32)
            terms.append(term * (dst >= 0).astype(jnp.float32))
        for t in range(slots):
            at = lanes(src_ref[0, o, t], size)
            total[:, at] = total[:, at] + terms[t]
        return carry

    lax.fori_loop(0, owners, owner, 0)
    out_ref[...] = total[:, :nodes]
    hub_ref[...] = total[:, nodes:].astype(hub_ref.dtype)


def pick_hubs(ids_ref, features_ref, out_ref):
    hubs = ids_ref.shape[1]
    size = out_ref.shape[1] // hubs
    for k in range(hubs):
        out_ref[:, k * size : (k + 1) * size] = features_ref[:, lanes(ids_ref[0, k], size)]


def add_hubs(ids_ref, part_ref, hub_ref, out_ref):
    peers, _, width = hub_ref.shape
    hubs = ids_ref.shape[1]
    size = width // hubs
    out_ref[...] = part_ref[...]
    back = hub_ref[0].astype(jnp.float32)
    for p in range(1, peers):
        back += hub_ref[p].astype(jnp.float32)
    for k in range(hubs):
        at = lanes(ids_ref[0, k], size)
        out_ref[:, at] = out_ref[:, at] + back[:, k * size : (k + 1) * size]


def exchange_body(axis, cuts, joins, *refs):
    items = len(cuts)
    inputs, outputs, held = refs[:items], refs[items : 2 * items], refs[2 * items : 3 * items]
    send_sem, recv_sem = refs[3 * items :]
    peers = lax.axis_size(axis)
    me = lax.axis_index(axis)

    def block(i, peer):
        if cuts[i] == "whole":
            return inputs[i]
        if cuts[i] == "lead":
            return inputs[i].at[peer]
        return inputs[i].at[:, lanes(peer, held[i].shape[2])]

    others = [lax.rem(me + step, peers) for step in range(1, peers)]
    barrier = pltpu.get_barrier_semaphore()
    for peer in others:
        pl.semaphore_signal(
            barrier, inc=1, device_id={axis: peer}, device_id_type=pl.DeviceIdType.MESH
        )
    pl.semaphore_wait(barrier, peers - 1)
    copies = []
    for i in range(items):
        for step, peer in enumerate(others):
            copy = pltpu.make_async_remote_copy(
                src_ref=block(i, peer),
                dst_ref=held[i].at[me],
                send_sem=send_sem.at[i, step],
                recv_sem=recv_sem.at[i, step],
                device_id={axis: peer},
                device_id_type=pl.DeviceIdType.MESH,
            )
            copy.start()
            copies.append(copy)
    for i in range(items):
        held[i][me] = block(i, me)[...]
    for copy in copies:
        copy.wait()
    for i in range(items):
        if joins[i] == "sum":
            total = held[i][0].astype(jnp.float32)
            for p in range(1, peers):
                total += held[i][p].astype(jnp.float32)
            outputs[i][...] = total
        elif joins[i] == "lanes":
            width = held[i].shape[2]
            for p in range(peers):
                outputs[i][:, p * width : (p + 1) * width] = held[i][p]
        else:
            outputs[i][...] = held[i][...]


def exchange(axis, number, arrays, cuts, joins):
    peers = lax.axis_size(axis)
    blocks, outs = [], []
    for array, cut, join in zip(arrays, cuts, joins):
        if cut == "lead":
            rows, width = array.shape[1:]
        else:
            rows, width = array.shape
            width = width // peers if cut == "lanes" else width
        blocks.append(pltpu.VMEM((peers, rows, width), array.dtype))
        shape = {"sum": (rows, width), "lanes": (rows, peers * width)}.get(join, (peers, rows, width))
        outs.append(jax.ShapeDtypeStruct(shape, jnp.float32 if join == "sum" else array.dtype))
    vmem = pl.BlockSpec(memory_space=pltpu.VMEM)
    semaphores = pltpu.SemaphoreType.DMA((len(arrays), peers - 1))
    return pl.pallas_call(
        functools.partial(exchange_body, axis, cuts, joins),
        out_shape=outs,
        in_specs=[vmem] * len(arrays),
        out_specs=[vmem] * len(arrays),
        scratch_shapes=[*blocks, semaphores, semaphores],
        compiler_params=pltpu.CompilerParams(
            collective_id=number, has_side_effects=True, vmem_limit_bytes=40 * 1024 * 1024
        ),
        name=f"exchange_{number}",
    )(*arrays)


def local(
    features,
    w_self,
    w_neigh,
    bias,
    tile_vals,
    tile_src,
    tile_dst,
    tile_count,
    hub_blocks,
    cotangent,
):
    columns, nodes = features.shape
    owners = lax.axis_size("feat")
    size = tile_vals.shape[-1]
    own_blocks = nodes // size // owners
    hidden = w_self.shape[1]
    rows = max(columns, 16)
    vmem, smem = pl.BlockSpec(memory_space=pltpu.VMEM), pl.BlockSpec(memory_space=pltpu.SMEM)
    params = pltpu.CompilerParams(vmem_limit_bytes=40 * 1024 * 1024)

    def padded(a):
        spare = [(0, 0)] * a.ndim
        spare[-2] = (0, rows - columns)
        return a if rows == columns else jnp.pad(a, spare)

    mine = padded(features)
    own_hubs = pl.pallas_call(
        pick_hubs,
        out_shape=jax.ShapeDtypeStruct((rows, hub_blocks.shape[1] * size), mine.dtype),
        in_specs=[smem, vmem],
        out_specs=vmem,
        compiler_params=params,
        name="pick_hubs",
    )(hub_blocks, mine)
    (all_hubs,) = exchange("grp", 0, [own_hubs], ["whole"], ["lanes"])
    slot_nodes = nodes + all_hubs.shape[1]
    both = pl.pallas_call(
        functools.partial(gather_tiles, own_blocks),
        out_shape=jax.ShapeDtypeStruct((2 * rows, nodes), jnp.bfloat16),
        in_specs=[smem, smem, smem, vmem, vmem, vmem],
        out_specs=vmem,
        scratch_shapes=[pltpu.VMEM((rows, slot_nodes), jnp.bfloat16)],
        compiler_params=params,
        name="gather_tiles",
    )(tile_src, tile_dst, tile_count, mine, all_hubs, tile_vals)
    (both,) = exchange("feat", 1, [both], ["lanes"], ["lead"])
    both = both.reshape(owners * 2 * rows, nodes // owners)
    weights = jnp.stack(
        [padded(w.reshape(owners, columns, hidden)) for w in (w_self, w_neigh)], axis=1
    ).reshape(owners * 2 * rows, hidden)
    preact = (
        lax.dot_general(both, weights, (((0,), (0,)), ((), ())), preferred_element_type=jnp.float32)
        + bias
    )
    sig = jax.nn.sigmoid(preact)
    output = (preact * sig).astype(jnp.bfloat16)
    slope = sig * (1.0 + preact * (1.0 - sig))
    grad_pre = (cotangent.astype(jnp.float32) * slope).astype(jnp.bfloat16)
    grads = lax.dot_general(
        weights, grad_pre, (((1,), (1,)), ((), ())), preferred_element_type=jnp.float32
    ).astype(jnp.bfloat16)
    weight_part = jnp.dot(both, grad_pre, preferred_element_type=jnp.float32)
    bias_part = jnp.sum(grad_pre.astype(jnp.float32), axis=0)
    sums = jnp.concatenate(
        [
            weight_part.reshape(owners, 2 * rows, hidden),
            jnp.broadcast_to(bias_part, (owners, 16, hidden)),
        ],
        axis=1,
    ).astype(jnp.bfloat16)
    back, sums = exchange(
        "feat",
        2,
        [grads.reshape(owners, 2 * rows, nodes // owners), sums],
        ["lead", "lead"],
        ["lanes", "sum"],
    )
    part, hub_part = pl.pallas_call(
        functools.partial(scatter_tiles, own_blocks),
        out_shape=(
            jax.ShapeDtypeStruct((rows, nodes), jnp.float32),
            jax.ShapeDtypeStruct((rows, slot_nodes - nodes), jnp.bfloat16),
        ),
        in_specs=[smem, smem, smem, vmem, vmem],
        out_specs=(vmem, vmem),
        scratch_shapes=[pltpu.VMEM((rows, slot_nodes), jnp.float32)],
        compiler_params=params,
        name="scatter_tiles",
    )(tile_src, tile_dst, tile_count, back, tile_vals)
    hub_back, sums = exchange("grp", 3, [hub_part, sums], ["lanes", "whole"], ["lead", "sum"])
    feat_grad = pl.pallas_call(
        add_hubs,
        out_shape=jax.ShapeDtypeStruct((columns, nodes), jnp.float32),
        in_specs=[smem, vmem, vmem],
        out_specs=vmem,
        compiler_params=params,
        name="add_hubs",
    )(hub_blocks, part[:columns], hub_back[:, :columns])
    return (
        output,
        feat_grad,
        sums[:columns],
        sums[rows : rows + columns],
        sums[2 * rows],
    )


def solution(mesh):
    return jax.shard_map(
        local,
        mesh=mesh,
        in_specs=(
            P("feat", "grp"),
            P(),
            P(),
            P(),
            P("grp", None, None, None, None),
            P("grp", None, None),
            P("grp", None, None),
            P("grp", None),
            P("grp", None),
            P(("grp", "feat"), None),
        ),
        out_specs=(
            P(("grp", "feat"), None),
            P("feat", "grp"),
            P("feat", None),
            P("feat", None),
            P(),
        ),
        check_vma=False,
    )
```

```python
import functools

import jax
import jax.numpy as jnp
from jax import lax
from jax.experimental import pallas as pl
from jax.experimental.pallas import tpu as pltpu
from jax.sharding import PartitionSpec as P


def lanes(index, width):
    return pl.ds(pl.multiple_of(index * width, width), width)


def destination(dst_ref, count_ref, o, t):
    return jnp.where(t < count_ref[0, o], dst_ref[0, o, t], -1)


def gather_tiles(
    own_blocks, src_ref, dst_ref, count_ref, features_ref, hubs_ref, tiles_ref, out_ref, x_ref
):
    _, owners, slots, size, _ = tiles_ref.shape
    rows = x_ref.shape[0]
    nodes = out_ref.shape[1]
    out_ref[:rows, :] = features_ref[...]
    x_ref[:, :nodes] = features_ref[...]
    x_ref[:, nodes:] = hubs_ref[...]

    def owner(o, carry):
        total = jnp.zeros((own_blocks * rows, size), jnp.float32)
        for t in range(slots):
            x = x_ref[:, lanes(src_ref[0, o, t], size)].astype(jnp.float32)
            dst = destination(dst_ref, count_ref, o, t)
            left = jnp.concatenate(
                [x * (dst == d).astype(jnp.float32) for d in range(own_blocks)], axis=0
            ).astype(jnp.bfloat16)
            total += lax.dot_general(
                left, tiles_ref[0, o, t], (((1,), (1,)), ((), ())), preferred_element_type=jnp.float32
            )
        for d in range(own_blocks):
            out_ref[rows:, lanes(o * own_blocks + d, size)] = total[d * rows : (d + 1) * rows].astype(
                out_ref.dtype
            )
        return carry

    lax.fori_loop(0, owners, owner, 0)


def scatter_tiles(own_blocks, src_ref, dst_ref, count_ref, g_ref, tiles_ref, out_ref, hub_ref, total):
    _, owners, slots, size, _ = tiles_ref.shape
    rows, nodes = out_ref.shape
    total[:, :nodes] = g_ref[:rows, :].astype(jnp.float32)
    total[:, nodes:] = jnp.zeros((total.shape[0], total.shape[1] - nodes), jnp.float32)

    def owner(o, carry):
        terms = []
        for t in range(slots):
            dst = destination(dst_ref, count_ref, o, t)
            g = g_ref[rows:, lanes(o * own_blocks + jnp.maximum(dst, 0), size)]
            term = jnp.dot(g, tiles_ref[0, o, t], preferred_element_type=jnp.float32)
            terms.append(term * (dst >= 0).astype(jnp.float32))
        for t in range(slots):
            at = lanes(src_ref[0, o, t], size)
            total[:, at] = total[:, at] + terms[t]
        return carry

    lax.fori_loop(0, owners, owner, 0)
    out_ref[...] = total[:, :nodes]
    hub_ref[...] = total[:, nodes:].astype(hub_ref.dtype)


def pick_hubs(ids_ref, features_ref, out_ref):
    hubs = ids_ref.shape[1]
    size = out_ref.shape[1] // hubs
    for k in range(hubs):
        out_ref[:, k * size : (k + 1) * size] = features_ref[:, lanes(ids_ref[0, k], size)]


def add_hubs(ids_ref, part_ref, hub_ref, out_ref):
    peers, _, width = hub_ref.shape
    hubs = ids_ref.shape[1]
    size = width // hubs
    out_ref[...] = part_ref[...]
    back = hub_ref[0].astype(jnp.float32)
    for p in range(1, peers):
        back += hub_ref[p].astype(jnp.float32)
    for k in range(hubs):
        at = lanes(ids_ref[0, k], size)
        out_ref[:, at] = out_ref[:, at] + back[:, k * size : (k + 1) * size]


def exchange_body(axis, cuts, joins, *refs):
    items = len(cuts)
    inputs, outputs, held = refs[:items], refs[items : 2 * items], refs[2 * items : 3 * items]
    send_sem, recv_sem = refs[3 * items :]
    peers = lax.axis_size(axis)
    me = lax.axis_index(axis)

    def block(i, peer):
        if cuts[i] == "whole":
            return inputs[i]
        if cuts[i] == "lead":
            return inputs[i].at[peer]
        return inputs[i].at[:, lanes(peer, held[i].shape[2])]

    steps = sorted(range(1, peers), key=lambda step: abs(2 * step - peers))
    others = [lax.rem(me + step, peers) for step in steps]
    barrier = pltpu.get_barrier_semaphore()
    for peer in others:
        pl.semaphore_signal(
            barrier, inc=1, device_id={axis: peer}, device_id_type=pl.DeviceIdType.MESH
        )
    pl.semaphore_wait(barrier, peers - 1)
    copies = []
    for i in range(items):
        for step, peer in enumerate(others):
            copy = pltpu.make_async_remote_copy(
                src_ref=block(i, peer),
                dst_ref=held[i].at[me],
                send_sem=send_sem.at[i, step],
                recv_sem=recv_sem.at[i, step],
                device_id={axis: peer},
                device_id_type=pl.DeviceIdType.MESH,
            )
            copy.start()
            copies.append(copy)
    for i in range(items):
        held[i][me] = block(i, me)[...]
    for copy in copies:
        copy.wait()
    for i in range(items):
        if joins[i] == "sum":
            total = held[i][0].astype(jnp.float32)
            for p in range(1, peers):
                total += held[i][p].astype(jnp.float32)
            outputs[i][...] = total
        elif joins[i] == "lanes":
            width = held[i].shape[2]
            for p in range(peers):
                outputs[i][:, p * width : (p + 1) * width] = held[i][p]
        else:
            outputs[i][...] = held[i][...]


def exchange(axis, number, arrays, cuts, joins):
    peers = lax.axis_size(axis)
    blocks, outs = [], []
    for array, cut, join in zip(arrays, cuts, joins):
        if cut == "lead":
            rows, width = array.shape[1:]
        else:
            rows, width = array.shape
            width = width // peers if cut == "lanes" else width
        blocks.append(pltpu.VMEM((peers, rows, width), array.dtype))
        shape = {"sum": (rows, width), "lanes": (rows, peers * width)}.get(join, (peers, rows, width))
        outs.append(jax.ShapeDtypeStruct(shape, jnp.float32 if join == "sum" else array.dtype))
    vmem = pl.BlockSpec(memory_space=pltpu.VMEM)
    semaphores = pltpu.SemaphoreType.DMA((len(arrays), peers - 1))
    return pl.pallas_call(
        functools.partial(exchange_body, axis, cuts, joins),
        out_shape=outs,
        in_specs=[vmem] * len(arrays),
        out_specs=[vmem] * len(arrays),
        scratch_shapes=[*blocks, semaphores, semaphores],
        compiler_params=pltpu.CompilerParams(
            collective_id=number, has_side_effects=True, vmem_limit_bytes=40 * 1024 * 1024
        ),
        name=f"exchange_{number}",
    )(*arrays)


def local(
    features,
    w_self,
    w_neigh,
    bias,
    tile_vals,
    tile_src,
    tile_dst,
    tile_count,
    hub_blocks,
    cotangent,
):
    columns, nodes = features.shape
    owners = lax.axis_size("feat")
    size = tile_vals.shape[-1]
    own_blocks = nodes // size // owners
    hidden = w_self.shape[1]
    rows = max(columns, 16)
    vmem, smem = pl.BlockSpec(memory_space=pltpu.VMEM), pl.BlockSpec(memory_space=pltpu.SMEM)
    params = pltpu.CompilerParams(vmem_limit_bytes=40 * 1024 * 1024)

    def padded(a):
        spare = [(0, 0)] * a.ndim
        spare[-2] = (0, rows - columns)
        return a if rows == columns else jnp.pad(a, spare)

    mine = padded(features)
    own_hubs = pl.pallas_call(
        pick_hubs,
        out_shape=jax.ShapeDtypeStruct((rows, hub_blocks.shape[1] * size), mine.dtype),
        in_specs=[smem, vmem],
        out_specs=vmem,
        compiler_params=params,
        name="pick_hubs",
    )(hub_blocks, mine)
    (all_hubs,) = exchange("grp", 0, [own_hubs], ["whole"], ["lanes"])
    slot_nodes = nodes + all_hubs.shape[1]
    both = pl.pallas_call(
        functools.partial(gather_tiles, own_blocks),
        out_shape=jax.ShapeDtypeStruct((2 * rows, nodes), jnp.bfloat16),
        in_specs=[smem, smem, smem, vmem, vmem, vmem],
        out_specs=vmem,
        scratch_shapes=[pltpu.VMEM((rows, slot_nodes), jnp.bfloat16)],
        compiler_params=params,
        name="gather_tiles",
    )(tile_src, tile_dst, tile_count, mine, all_hubs, tile_vals)
    (both,) = exchange("feat", 1, [both], ["lanes"], ["lead"])
    both = both.reshape(owners * 2 * rows, nodes // owners)
    weights = jnp.stack(
        [padded(w.reshape(owners, columns, hidden)) for w in (w_self, w_neigh)], axis=1
    ).reshape(owners * 2 * rows, hidden)
    preact = (
        lax.dot_general(both, weights, (((0,), (0,)), ((), ())), preferred_element_type=jnp.float32)
        + bias
    )
    sig = jax.nn.sigmoid(preact)
    output = (preact * sig).astype(jnp.bfloat16)
    slope = sig * (1.0 + preact * (1.0 - sig))
    grad_pre = (cotangent.astype(jnp.float32) * slope).astype(jnp.bfloat16)
    grads = lax.dot_general(
        weights, grad_pre, (((1,), (1,)), ((), ())), preferred_element_type=jnp.float32
    ).astype(jnp.bfloat16)
    weight_part = jnp.dot(both, grad_pre, preferred_element_type=jnp.float32)
    bias_part = jnp.sum(grad_pre.astype(jnp.float32), axis=0)
    sums = jnp.concatenate(
        [
            weight_part.reshape(owners, 2 * rows, hidden),
            jnp.broadcast_to(bias_part, (owners, 16, hidden)),
        ],
        axis=1,
    ).astype(jnp.bfloat16)
    back, sums = exchange(
        "feat",
        2,
        [grads.reshape(owners, 2 * rows, nodes // owners), sums],
        ["lead", "lead"],
        ["lanes", "sum"],
    )
    part, hub_part = pl.pallas_call(
        functools.partial(scatter_tiles, own_blocks),
        out_shape=(
            jax.ShapeDtypeStruct((rows, nodes), jnp.float32),
            jax.ShapeDtypeStruct((rows, slot_nodes - nodes), jnp.bfloat16),
        ),
        in_specs=[smem, smem, smem, vmem, vmem],
        out_specs=(vmem, vmem),
        scratch_shapes=[pltpu.VMEM((rows, slot_nodes), jnp.float32)],
        compiler_params=params,
        name="scatter_tiles",
    )(tile_src, tile_dst, tile_count, back, tile_vals)
    hub_back, sums = exchange("grp", 3, [hub_part, sums], ["lanes", "whole"], ["lead", "sum"])
    feat_grad = pl.pallas_call(
        add_hubs,
        out_shape=jax.ShapeDtypeStruct((columns, nodes), jnp.float32),
        in_specs=[smem, vmem, vmem],
        out_specs=vmem,
        compiler_params=params,
        name="add_hubs",
    )(hub_blocks, part[:columns], hub_back[:, :columns])
    return (
        output,
        feat_grad,
        sums[:columns],
        sums[rows : rows + columns],
        sums[2 * rows],
    )


def solution(mesh):
    return jax.shard_map(
        local,
        mesh=mesh,
        in_specs=(
            P("feat", "grp"),
            P(),
            P(),
            P(),
            P("grp", None, None, None, None),
            P("grp", None, None),
            P("grp", None, None),
            P("grp", None),
            P("grp", None),
            P(("grp", "feat"), None),
        ),
        out_specs=(
            P(("grp", "feat"), None),
            P("feat", "grp"),
            P("feat", None),
            P("feat", None),
            P(),
        ),
        check_vma=False,
    )
```
